32 devices in a mesh: ctx: 4 (over y, core), head: 2 (over x), rep: 4 (over z).
Axes of the slice: x: 2, y: 2, z: 4, core: 2. Of those that a mesh axis runs over, the one named last changes fastest.
Arguments:
- q_turn: bfloat16 [1024, 8192], P(('rep', 'ctx', 'head')), parts along dimension 0, may hold values from -18 to 18
- k_turn: bfloat16 [1024, 1024], P(('rep', 'ctx', 'head')), parts along dimension 0, may hold values from -6 to 6
- v_turn: bfloat16 [1024, 1024], P(('rep', 'ctx', 'head')), parts along dimension 0, may hold values from -6 to 6
- cache_k: bfloat16 [512, 64, 1024], P(('rep', 'ctx'), None, 'head'), parts along dimension 0, may hold values from -6 to 6
- cache_v: bfloat16 [512, 64, 1024], P(('rep', 'ctx'), None, 'head'), parts along dimension 0, may hold values from -6 to 6
- k_scale: float32 [512, 8], P(('rep', 'ctx'), 'head'), parts along dimension 0, may hold values from 0.25 to 2
- v_scale: float32 [512, 8], P(('rep', 'ctx'), 'head'), parts along dimension 0, may hold values from 0.25 to 2
- page_map: int32 [512], P(('rep', 'ctx')), parts along dimension 0, may hold values from 0 to 127, as said below
Outputs:
- attn_out: bfloat16 [1024, 8192], P(('rep', 'ctx'), 'head'), parts along dimension 0
- cache_k_paired: bfloat16 [32768, 1024], P(('rep', 'ctx'), 'head'), parts along dimension 0
- cache_v_paired: bfloat16 [32768, 1024], P(('rep', 'ctx'), 'head'), parts along dimension 0
The draws below stay inside these ranges and needn't reach their ends.
There are 4 independent parts, one for each index of `rep`. The reference program is written for one: setup_inputs(seed, part) draws one part's arguments, and reference() takes and returns one part's arrays. A program takes and returns all parts, laid end to end along the dimension named above; each array names one. Nothing has to cross between parts.
Inputs may be any that keep to these rules, and one draw needn't show every extreme that they name: A permutation: slot s holds logical page page_map[s]. Cut the 128 logical pages into 8 blocks of 16 consecutive pages; the 32 slots of each index of ctx hold exactly one page of every block.
All inputs are finite; a program needn't handle non-finite values.
Results may differ from the reference program's by a relative error of at most 0.0087.
Values may be sent and summed in bfloat16 or wider, within the bound.
A program may use at most 128 MiB of HBM per device.

```python
import math
import jax
import jax.numpy as jnp
from jax import lax

HQ = 64
KVH = 8
HD = 128
PAGE = 64
TURN = 256
PG_DEV = 32
PAGES = 128
CACHE = 8192
N_CTX = 4


def turn_arrays(key):
    base = jax.random.fold_in(key, 21)
    key_query, key_keys = jax.random.split(base, 2)
    queries = jax.random.truncated_normal(key_query, -6.0, 6.0, (TURN, HQ * HD), jnp.float32)
    turn_keys = jax.random.truncated_normal(key_keys, -6.0, 6.0, (TURN, KVH * HD), jnp.float32)
    return (queries, turn_keys)


def draw_q_turn(key, part):
    queries, turn_keys = turn_arrays(key)
    return queries.astype(jnp.bfloat16)


def draw_k_turn(key, part):
    queries, turn_keys = turn_arrays(key)
    return turn_keys.astype(jnp.bfloat16)


def one_ranking(block_key):
    return jax.random.permutation(block_key, PG_DEV // 2)


def draw_page_map(key, part):
    per_device = PG_DEV // (2 * N_CTX)
    block_keys = jax.random.split(jax.random.fold_in(key, 11), 2 * N_CTX)
    ranks = jax.vmap(one_ranking)(block_keys)
    holder = (ranks // per_device).reshape(PAGES).astype(jnp.int32)
    breaker = jax.random.permutation(jax.random.fold_in(key, 12), PAGES).astype(jnp.int32)
    return jnp.argsort(holder * PAGES + breaker).astype(jnp.int32)


def levels(own_key, shape, shards, smallest, top_value):
    def one(position, shards_of):
        heights = jax.random.uniform(jax.random.fold_in(jax.random.fold_in(own_key, 6), position), (shards_of,), jnp.float32, smallest / len(shards), top_value / len(shards))
        return jnp.repeat(jnp.exp(heights), shape[position] // shards_of).reshape((-1,) + (1,) * (len(shape) - position - 1))

    loudness = one(*shards[0])
    for cut in shards[1:]:
        loudness = loudness * one(*cut)
    return loudness


def normal_values(key, shape, scale, bound, cuts=(), kind=jnp.bfloat16):
    result = scale * jax.random.normal(key, shape, jnp.float32)
    if cuts:
        result = result * levels(key, shape, cuts, -0.22, 0.18)
    return jnp.clip(result, -bound, bound).astype(kind)


def setup_inputs(seed: int = 0, part: int = 0) -> dict:
    keys = jax.random.split(jax.random.key(seed), 9)
    part_splits = jax.random.split(jax.random.fold_in(keys[8], part), 9)
    return {
        "q_turn": draw_q_turn(jax.random.fold_in(jax.random.fold_in(keys[8], part), 71), part),
        "k_turn": draw_k_turn(jax.random.fold_in(jax.random.fold_in(keys[8], part), 71), part),
        "v_turn": normal_values(part_splits[2], (TURN, KVH * HD), 1.0, 6.0, ((0, 8),)),
        "cache_k": normal_values(part_splits[3], (PAGES, PAGE, KVH * HD), 1.0, 6.0, ((0, 4), (2, 2))),
        "cache_v": normal_values(part_splits[4], (PAGES, PAGE, KVH * HD), 1.0, 6.0, ((0, 4), (2, 2))),
        "k_scale": jnp.clip(jnp.exp(math.log(2.0) - 2.0794415 * jax.random.uniform(part_splits[5], (PAGES, KVH), jnp.float32) ** levels(part_splits[5], (PAGES, KVH), ((0, 4), (1, 2)), -0.2, 0.2)), 0.25, 2.0),
        "v_scale": jnp.clip(jnp.exp(math.log(2.0) - 2.0794415 * jax.random.uniform(part_splits[6], (PAGES, KVH), jnp.float32) ** levels(part_splits[6], (PAGES, KVH), ((0, 4), (1, 2)), -0.2, 0.2)), 0.25, 2.0),
        "page_map": draw_page_map(jax.random.fold_in(jax.random.fold_in(keys[8], part), 71), part),
    }


def scale_pages(codes, scales):
    full = codes.astype(jnp.float32).reshape(PAGES, PAGE, KVH, HD) * scales[:, None, :, None]
    return full.reshape(PAGES, PAGE, KVH * HD).astype(jnp.bfloat16)

def reference(q_turn, k_turn, v_turn, cache_k, cache_v, k_scale, v_scale, page_map):
    inverse = jnp.argsort(page_map)
    logical_k = scale_pages(cache_k, k_scale)[inverse].reshape(CACHE, KVH * HD)
    logical_v = scale_pages(cache_v, v_scale)[inverse].reshape(CACHE, KVH * HD)
    blocks = 2 * N_CTX
    block_rows = CACHE // blocks
    lower = jnp.arange(N_CTX)
    order = jnp.stack([lower, blocks - 1 - lower], axis=1).reshape(blocks)
    paired_k = logical_k.reshape(blocks, block_rows, KVH * HD)[order].reshape(CACHE, KVH * HD)
    paired_v = logical_v.reshape(blocks, block_rows, KVH * HD)[order].reshape(CACHE, KVH * HD)
    per_group = HQ // KVH
    factor = 1.0 / math.sqrt(HD)
    by_head = q_turn.reshape(TURN, HQ, HD).transpose(1, 0, 2)
    cache_kh = logical_k.reshape(CACHE, KVH, HD)
    cache_vh = logical_v.reshape(CACHE, KVH, HD)
    turn_kh = k_turn.reshape(TURN, KVH, HD)
    turn_vh = v_turn.reshape(TURN, KVH, HD)
    visible = jnp.arange(TURN)[None, :] <= jnp.arange(TURN)[:, None]
    dims = (((1,), (1,)), ((), ()))

    def one_head(pair):
        query, index = pair
        kv_index = index // per_group
        ck = lax.dynamic_index_in_dim(cache_kh, kv_index, 1, keepdims=False)
        cv = lax.dynamic_index_in_dim(cache_vh, kv_index, 1, keepdims=False)
        tk = lax.dynamic_index_in_dim(turn_kh, kv_index, 1, keepdims=False)
        tv = lax.dynamic_index_in_dim(turn_vh, kv_index, 1, keepdims=False)
        cached = lax.dot_general(query, ck, dims, preferred_element_type=jnp.float32) * factor
        recent = lax.dot_general(query, tk, dims, preferred_element_type=jnp.float32) * factor
        recent = jnp.where(visible, recent, -jnp.inf)
        peak = jnp.maximum(lax.optimization_barrier(jnp.max(cached, axis=1)), lax.optimization_barrier(jnp.max(recent, axis=1)))
        cached_e = jnp.exp(cached - peak[:, None])
        recent_e = jnp.exp(recent - peak[:, None])
        total = lax.optimization_barrier(jnp.sum(cached_e, axis=1)) + lax.optimization_barrier(jnp.sum(recent_e, axis=1))
        mixed = jnp.dot(cached_e.astype(jnp.bfloat16), cv, preferred_element_type=jnp.float32)
        mixed = mixed + jnp.dot(recent_e.astype(jnp.bfloat16), tv, preferred_element_type=jnp.float32)
        return mixed / total[:, None]
    heads_out = lax.map(one_head, (by_head, jnp.arange(HQ, dtype=jnp.int32)))
    attn_out = heads_out.transpose(1, 0, 2).reshape(TURN, HQ * HD).astype(jnp.bfloat16)
    return (attn_out, paired_k, paired_v)
```

```python
import functools
import math

import jax
import jax.numpy as jnp
from jax import lax
from jax.experimental import pallas as pl
from jax.experimental.pallas import tpu as pltpu
from jax.sharding import PartitionSpec as P

MESH = pl.DeviceIdType.MESH
NT = (((1,), (1,)), ((), ()))


def main_kernel(
    n,
    heads,
    head_dim,
    order,
    k_scale,
    v_scale,
    page_map,
    q_turn,
    k_turn,
    v_turn,
    cache_k,
    cache_v,
    out,
    recv_k,
    recv_v,
    maps,
    raw_k,
    raw_v,
    sent_k,
    sent_v,
    q_all,
    k_mine,
    v_mine,
    acc,
    stats,
    sib_acc,
    sib_stats,
    far_out,
    far_out_stats,
    far_in,
    far_in_stats,
    local_sem,
    swap_send,
    swap_recv,
    far_q_send,
    far_q_recv,
    near_q_send,
    near_q_recv,
    page_send,
    page_recv,
    map_send,
    map_recv,
    near_send,
    near_recv,
    far_send,
    far_recv,
):
    c = lax.axis_index("ctx")
    h = lax.axis_index("head")
    chips = n // 2
    chip, core = c // 2, c % 2
    sibling = chip * 2 + (1 - core)
    slots, page_rows, width = raw_k.shape
    per_peer = slots // n
    part_rows, q_width = q_all.shape[2], q_all.shape[3]
    rows = heads * part_rows
    kv_heads = width // head_dim
    q_heads = q_width // head_dim
    per_group = q_heads // kv_heads
    factor = 1.0 / math.sqrt(head_dim)

    def remote(src, dst, send, recv, **where):
        return pltpu.make_async_remote_copy(
            src_ref=src,
            dst_ref=dst,
            send_sem=send,
            recv_sem=recv,
            device_id=where,
            device_id_type=MESH,
        )

    def same_core(d):
        return lax.rem(chip + d, chips) * 2 + core

    def other_core(d):
        return lax.rem(chip + d, chips) * 2 + (1 - core)

    pages_in = [
        pltpu.make_async_copy(cache_k, raw_k, local_sem.at[0]),
        pltpu.make_async_copy(cache_v, raw_v, local_sem.at[1]),
    ]
    for copy in pages_in:
        copy.start()
    own_turn = [
        pltpu.make_async_copy(
            src.at[:, pl.ds(pl.multiple_of(h * size, size), size)], dst, local_sem.at[2 + i]
        )
        for i, (src, dst, size) in enumerate(
            (
                (q_turn, q_all.at[c, h], q_width),
                (k_turn, k_mine.at[h], width),
                (v_turn, v_mine.at[h], width),
            )
        )
    ]
    for copy in own_turn:
        copy.start()

    barrier = pltpu.get_barrier_semaphore()
    for e in range(1, n):
        pl.semaphore_signal(
            barrier, inc=1, device_id={"ctx": lax.rem(c + e, n)}, device_id_type=MESH
        )
    for e in range(1, heads):
        pl.semaphore_signal(
            barrier, inc=1, device_id={"head": lax.rem(h + e, heads)}, device_id_type=MESH
        )
    pl.semaphore_wait(barrier, n - 1 + heads - 1)

    swaps = []
    for e in range(1, heads):
        peer = lax.rem(h + e, heads)
        for i, (src, dst, size) in enumerate(
            (
                (q_turn, q_all.at[c, h], q_width),
                (k_turn, k_mine.at[h], width),
                (v_turn, v_mine.at[h], width),
            )
        ):
            swaps.append(
                remote(
                    src.at[:, pl.ds(pl.multiple_of(peer * size, size), size)],
                    dst,
                    swap_send.at[i, e - 1],
                    swap_recv.at[i, e - 1],
                    head=peer,
                )
            )
    for copy in swaps:
        copy.start()
    map_copies = [
        remote(page_map, maps.at[c], map_send.at[e - 1], map_recv.at[e - 1], ctx=lax.rem(c + e, n))
        for e in range(1, n)
    ]
    for copy in map_copies:
        copy.start()
    own_map = pltpu.make_async_copy(page_map, maps.at[c], local_sem.at[5])
    own_map.start()
    for copy in own_turn:
        copy.wait()
    for copy in swaps:
        copy.wait()

    far_q = [
        remote(q_all.at[c], q_all.at[c], far_q_send.at[d - 1], far_q_recv.at[d - 1], ctx=same_core(d))
        for d in range(1, chips)
    ]
    for copy in far_q:
        copy.start()
    near_q = [
        remote(q_all.at[c], q_all.at[c], near_q_send.at[0], near_q_recv.at[0], ctx=sibling)
    ]
    near_q[0].start()

    for copy in pages_in:
        copy.wait()

    def scale_page(j, carry):
        slot = order[j]
        for raw, sent, scale in ((raw_k, sent_k, k_scale), (raw_v, sent_v, v_scale)):
            page = raw[slot]
            for g in range(kv_heads):
                columns = slice(g * head_dim, (g + 1) * head_dim)
                sent[j, :, columns] = (
                    page[:, columns].astype(jnp.float32) * scale[slot, g]
                ).astype(jnp.bfloat16)
        return carry

    lax.fori_loop(0, slots, scale_page, 0)

    for d in range(1, chips):
        far_q[d - 1].wait()
        source = lax.rem(chip + chips - d, chips) * 2 + core
        near_q.append(
            remote(
                q_all.at[source],
                q_all.at[source],
                near_q_send.at[d],
                near_q_recv.at[d],
                ctx=sibling,
            )
        )
        near_q[d].start()

    page_copies = []
    for e in range(1, n):
        peer = lax.rem(c + e, n)
        for i, (sent, recv) in enumerate(((sent_k, recv_k), (sent_v, recv_v))):
            page_copies.append(
                remote(
                    sent.at[pl.ds(peer * per_peer, per_peer)],
                    recv.at[c],
                    page_send.at[i, e - 1],
                    page_recv.at[i, e - 1],
                    ctx=peer,
                )
            )
    for copy in page_copies:
        copy.start()
    own_pages = [
        pltpu.make_async_copy(
            sent.at[pl.ds(c * per_peer, per_peer)], recv.at[c], local_sem.at[6 + i]
        )
        for i, (sent, recv) in enumerate(((sent_k, recv_k), (sent_v, recv_v)))
    ]
    for copy in own_pages:
        copy.start()

    at_once = max(1, min(per_group, 256 // rows))
    chunks = per_group // at_once
    lanes = lax.broadcasted_iota(jnp.int32, (rows, 128), 1)

    def flat(block):
        if part_rows % 16 == 0:
            return block.reshape(rows, block.shape[2])
        wide = block.astype(jnp.float32)
        return jnp.concatenate([wide[i] for i in range(heads)], axis=0).astype(jnp.bfloat16)

    def attend(block, g, chunk):
        first = g * per_group + chunk * at_once
        start = pl.multiple_of(first * head_dim, head_dim)
        own = pl.ds(pl.multiple_of(g * head_dim, head_dim), head_dim)
        q_block = flat(q_all[block, :, :, pl.ds(start, at_once * head_dim)])
        query = jnp.concatenate(
            [q_block[:, i * head_dim : (i + 1) * head_dim] for i in range(at_once)], axis=0
        )
        keys = sent_k[:, :, own].reshape(slots * page_rows, head_dim)
        values = sent_v[:, :, own].reshape(slots * page_rows, head_dim)
        turn_keys = flat(k_mine[:, :, own])
        turn_values = flat(v_mine[:, :, own])
        cached = lax.dot_general(query, keys, NT, preferred_element_type=jnp.float32) * factor
        recent = lax.dot_general(query, turn_keys, NT, preferred_element_type=jnp.float32) * factor
        line = lax.broadcasted_iota(jnp.int32, (at_once, rows, rows), 1).reshape(
            at_once * rows, rows
        )
        column = lax.broadcasted_iota(jnp.int32, (at_once * rows, rows), 1)
        visible = c * rows + column <= block * rows + line
        recent = jnp.where(visible, recent, -jnp.inf)
        peak = jnp.maximum(
            jnp.max(cached, axis=1, keepdims=True), jnp.max(recent, axis=1, keepdims=True)
        )
        cached = jnp.exp(cached - peak)
        recent = jnp.exp(recent - peak)
        total = jnp.sum(cached, axis=1, keepdims=True) + jnp.sum(recent, axis=1, keepdims=True)
        mixed = jnp.dot(
            cached.astype(jnp.bfloat16), values, preferred_element_type=jnp.float32
        ) + jnp.dot(recent.astype(jnp.bfloat16), turn_values, preferred_element_type=jnp.float32)
        kept = stats[block]
        for i in range(at_once):
            these = slice(i * rows, (i + 1) * rows)
            acc[block, :, pl.ds(pl.multiple_of(start + i * head_dim, head_dim), head_dim)] = mixed[
                these
            ]
            kept = jnp.where(lanes == first + i, peak[these], kept)
            kept = jnp.where(lanes == q_heads + first + i, total[these], kept)
        stats[block] = kept

    def attend_block(block):
        stats[block] = jnp.zeros((rows, 128), jnp.float32)

        def step(i, carry):
            attend(block, i // chunks, i % chunks)
            return carry

        lax.fori_loop(0, kv_heads * chunks, step, 0)

    near = []

    def give(d):
        block = other_core(d)
        for i, (src, dst) in enumerate(((acc, sib_acc), (stats, sib_stats))):
            copy = remote(
                src.at[block], dst.at[d], near_send.at[i, d], near_recv.at[i, d], ctx=sibling
            )
            copy.start()
            near.append(copy)

    attend_block(c)
    near_q[0].wait()
    attend_block(sibling)
    give(0)
    for d in range(1, chips):
        near_q[d].wait()

    def far_other(d, carry):
        attend_block(other_core(d))
        return carry

    def far_same(d, carry):
        attend_block(same_core(d))
        return carry

    lax.fori_loop(1, chips, far_other, 0)
    for d in range(1, chips):
        give(d)
    lax.fori_loop(1, chips, far_same, 0)

    def pick(stat, i):
        return stat[:, i : i + 1], stat[:, q_heads + i : q_heads + i + 1]

    def join(stats_a, read_a, stats_b, read_b, write):
        kept = jnp.zeros((rows, 128), jnp.float32)
        for i in range(q_heads):
            columns = slice(i * head_dim, (i + 1) * head_dim)
            peak_a, total_a = pick(stats_a, i)
            peak_b, total_b = pick(stats_b, i)
            peak = jnp.maximum(peak_a, peak_b)
            weight_a = jnp.exp(peak_a - peak)
            weight_b = jnp.exp(peak_b - peak)
            total = total_a * weight_a + total_b * weight_b
            mixed = read_a(columns) * weight_a + read_b(columns).astype(jnp.float32) * weight_b
            write(columns, mixed, total)
            kept = jnp.where(lanes == i, peak, kept)
            kept = jnp.where(lanes == q_heads + i, total, kept)
        return kept

    far = []
    for d in [*range(1, chips), 0]:
        near[2 * d].wait()
        near[2 * d + 1].wait()
        block = same_core(d)

        def write(columns, mixed, total, d=d):
            if d:
                far_out[d - 1, :, columns] = mixed.astype(jnp.bfloat16)
            elif chips == 1:
                out[:, columns] = (mixed / total).astype(jnp.bfloat16)
            else:
                acc[c, :, columns] = mixed

        kept = join(
            stats[block],
            lambda columns, block=block: acc[block, :, columns],
            sib_stats[d],
            lambda columns, d=d: sib_acc[d, :, columns],
            write,
        )
        if d:
            far_out_stats[d - 1] = kept
            for i, (src, dst) in enumerate(((far_out, far_in), (far_out_stats, far_in_stats))):
                copy = remote(
                    src.at[d - 1],
                    dst.at[d - 1],
                    far_send.at[i, d - 1],
                    far_recv.at[i, d - 1],
                    ctx=block,
                )
                copy.start()
                far.append(copy)
        else:
            stats[c] = kept

    for d in range(1, chips):
        far[2 * (d - 1)].wait()
        far[2 * (d - 1) + 1].wait()
        last = d == chips - 1

        def write_far(columns, mixed, total, last=last):
            if last:
                out[:, columns] = (mixed / total).astype(jnp.bfloat16)
            else:
                acc[c, :, columns] = mixed

        kept = join(
            stats[c],
            lambda columns: acc[c, :, columns],
            far_in_stats[d - 1],
            lambda columns, d=d: far_in[d - 1, :, columns],
            write_far,
        )
        if not last:
            stats[c] = kept

    own_map.wait()
    for copy in own_pages + map_copies + page_copies:
        copy.wait()


def place_kernel(n, maps, attn, recv_k, recv_v, out, out_k, out_v, sem):
    c = lax.axis_index("ctx")
    slots = out_k.shape[0]
    half = slots // 2
    passed = pltpu.make_async_copy(attn, out, sem.at[2])
    passed.start()
    for source in range(n):

        def visit(s, count, source=source):
            page = maps[source, 0, s]
            block = page // half
            within = page % half
            first = block == c
            mine = first | (block == 2 * n - 1 - c)

            @pl.when(mine)
            def _():
                place = jnp.where(first, within, half + within)
                for recv, to, i in ((recv_k, out_k, 0), (recv_v, out_v, 1)):
                    pltpu.make_async_copy(recv.at[source, count], to.at[place], sem.at[i]).start()

            return count + mine.astype(jnp.int32)

        lax.fori_loop(0, slots, visit, jnp.int32(0))
    passed.wait()
    for to, i in ((out_k, 0), (out_v, 1)):
        pltpu.make_async_copy(to, to, sem.at[i]).wait()


def local(q_turn, k_turn, v_turn, cache_k, cache_v, k_scale, v_scale, page_map):
    n = lax.axis_size("ctx")
    heads = lax.axis_size("head")
    slots, page_rows, width = cache_k.shape
    kv_heads = k_scale.shape[1]
    head_dim = width // kv_heads
    part_rows = q_turn.shape[0]
    rows = part_rows * heads
    q_width = q_turn.shape[1] // heads
    half = slots // 2
    per_peer = slots // n
    chips = n // 2
    bf16, f32 = jnp.bfloat16, jnp.float32

    block = page_map // half
    owner = jnp.where(block < n, block, 2 * n - 1 - block)
    slot = jnp.arange(slots, dtype=jnp.int32)
    before = (owner[None, :] == owner[:, None]) & (slot[None, :] < slot[:, None])
    rank = owner * per_peer + jnp.sum(before, axis=1, dtype=jnp.int32)
    order = jnp.sum(
        jnp.where(rank[None, :] == slot[:, None], slot[None, :], 0), axis=1, dtype=jnp.int32
    )
    map_row = jnp.pad(page_map, (0, -slots % 128))[None, :]

    smem = pl.BlockSpec(memory_space=pltpu.SMEM)
    vmem = pl.BlockSpec(memory_space=pltpu.VMEM)
    anywhere = pl.BlockSpec(memory_space=pl.ANY)
    dma = pltpu.SemaphoreType.DMA
    received = jax.ShapeDtypeStruct((n, per_peer, page_rows, width), bf16)
    some = max(1, chips - 1)
    keys = slots * page_rows + rows
    attn, recv_k, recv_v, maps = pl.pallas_call(
        functools.partial(main_kernel, n, heads, head_dim),
        out_shape=(
            jax.ShapeDtypeStruct((rows, q_width), bf16),
            received,
            received,
            jax.ShapeDtypeStruct((n, *map_row.shape), jnp.int32),
        ),
        in_specs=[smem] * 3 + [vmem] + [anywhere] * 5,
        out_specs=(vmem, anywhere, anywhere, vmem),
        scratch_shapes=[
            pltpu.VMEM((slots, page_rows, width), bf16),
            pltpu.VMEM((slots, page_rows, width), bf16),
            pltpu.VMEM((slots, page_rows, width), bf16),
            pltpu.VMEM((slots, page_rows, width), bf16),
            pltpu.VMEM((n, heads, part_rows, q_width), bf16),
            pltpu.VMEM((heads, part_rows, width), bf16),
            pltpu.VMEM((heads, part_rows, width), bf16),
            pltpu.VMEM((n, rows, q_width), f32),
            pltpu.VMEM((n, rows, 128), f32),
            pltpu.VMEM((chips, rows, q_width), f32),
            pltpu.VMEM((chips, rows, 128), f32),
            pltpu.VMEM((some, rows, q_width), bf16),
            pltpu.VMEM((some, rows, 128), f32),
            pltpu.VMEM((some, rows, q_width), bf16),
            pltpu.VMEM((some, rows, 128), f32),
            dma((8,)),
            dma((3, max(1, heads - 1))),
            dma((3, max(1, heads - 1))),
            dma((some,)),
            dma((some,)),
            dma((chips,)),
            dma((chips,)),
            dma((2, n - 1)),
            dma((2, n - 1)),
            dma((n - 1,)),
            dma((n - 1,)),
            dma((2, chips)),
            dma((2, chips)),
            dma((2, some)),
            dma((2, some)),
        ],
        compiler_params=pltpu.CompilerParams(
            collective_id=0, has_side_effects=True, vmem_limit_bytes=48 * 2**20
        ),
        cost_estimate=pl.CostEstimate(
            flops=4 * n * rows * q_width * keys,
            bytes_accessed=8 * slots * page_rows * width * 2,
            transcendentals=n * rows * (q_width // head_dim) * keys,
        ),
        name="exchange_and_attend",
    )(order, k_scale, v_scale, map_row, q_turn, k_turn, v_turn, cache_k, cache_v)

    paged = jax.ShapeDtypeStruct((slots, page_rows, width), bf16)
    attn_out, paired_k, paired_v = pl.pallas_call(
        functools.partial(place_kernel, n),
        out_shape=(jax.ShapeDtypeStruct((rows, q_width), bf16), paged, paged),
        in_specs=[smem, anywhere, anywhere, anywhere],
        out_specs=(anywhere, anywhere, anywhere),
        scratch_shapes=[dma((3,))],
        cost_estimate=pl.CostEstimate(
            flops=0, bytes_accessed=4 * slots * page_rows * width * 2, transcendentals=0
        ),
        name="place_pages",
    )(maps, attn, recv_k, recv_v)
    flat = (slots * page_rows, width)
    return (attn_out, paired_k.reshape(flat), paired_v.reshape(flat))


def solution(mesh):
    return jax.shard_map(
        local,
        mesh=mesh,
        in_specs=(
            P(("rep", "ctx", "head"), None),
            P(("rep", "ctx", "head"), None),
            P(("rep", "ctx", "head"), None),
            P(("rep", "ctx"), None, "head"),
            P(("rep", "ctx"), None, "head"),
            P(("rep", "ctx"), "head"),
            P(("rep", "ctx"), "head"),
            P(("rep", "ctx")),
        ),
        out_specs=(P(("rep", "ctx"), "head"), P(("rep", "ctx"), "head"), P(("rep", "ctx"), "head")),
        check_vma=False,
    )
```

```python
import functools
import math

import jax
import jax.numpy as jnp
from jax import lax
from jax.experimental import pallas as pl
from jax.experimental.pallas import tpu as pltpu
from jax.sharding import PartitionSpec as P

MESH = pl.DeviceIdType.MESH
NT = (((1,), (1,)), ((), ()))


def main_kernel(
    n,
    heads,
    head_dim,
    order,
    k_scale,
    v_scale,
    page_map,
    q_turn,
    k_turn,
    v_turn,
    cache_k,
    cache_v,
    out,
    recv_k,
    recv_v,
    maps,
    raw_k,
    raw_v,
    sent_k,
    sent_v,
    q_all,
    k_mine,
    v_mine,
    acc,
    stats,
    sib_acc,
    sib_stats,
    far_out,
    far_out_stats,
    far_in,
    far_in_stats,
    local_sem,
    swap_send,
    swap_recv,
    far_q_send,
    far_q_recv,
    near_q_send,
    near_q_recv,
    page_send,
    page_recv,
    map_send,
    map_recv,
    near_send,
    near_recv,
    far_send,
    far_recv,
):
    c = lax.axis_index("ctx")
    h = lax.axis_index("head")
    chips = n // 2
    chip, core = c // 2, c % 2
    sibling = chip * 2 + (1 - core)
    slots, page_rows, width = raw_k.shape
    per_peer = slots // n
    part_rows, q_width = q_all.shape[2], q_all.shape[3]
    rows = heads * part_rows
    kv_heads = width // head_dim
    q_heads = q_width // head_dim
    per_group = q_heads // kv_heads
    factor = math.log2(math.e) / math.sqrt(head_dim)

    def remote(src, dst, send, recv, **where):
        return pltpu.make_async_remote_copy(
            src_ref=src,
            dst_ref=dst,
            send_sem=send,
            recv_sem=recv,
            device_id=where,
            device_id_type=MESH,
        )

    def same_core(d):
        return lax.rem(chip + d, chips) * 2 + core

    def other_core(d):
        return lax.rem(chip + d, chips) * 2 + (1 - core)

    pages_in = [
        pltpu.make_async_copy(cache_k, raw_k, local_sem.at[0]),
        pltpu.make_async_copy(cache_v, raw_v, local_sem.at[1]),
    ]
    for copy in pages_in:
        copy.start()
    own_turn = [
        pltpu.make_async_copy(
            src.at[:, pl.ds(pl.multiple_of(h * size, size), size)], dst, local_sem.at[2 + i]
        )
        for i, (src, dst, size) in enumerate(
            (
                (q_turn, q_all.at[c, h], q_width),
                (k_turn, k_mine.at[h], width),
                (v_turn, v_mine.at[h], width),
            )
        )
    ]
    for copy in own_turn:
        copy.start()

    barrier = pltpu.get_barrier_semaphore()
    for e in range(1, n):
        pl.semaphore_signal(
            barrier, inc=1, device_id={"ctx": lax.rem(c + e, n)}, device_id_type=MESH
        )
    for e in range(1, heads):
        pl.semaphore_signal(
            barrier, inc=1, device_id={"head": lax.rem(h + e, heads)}, device_id_type=MESH
        )
    pl.semaphore_wait(barrier, n - 1 + heads - 1)

    swaps = []
    for e in range(1, heads):
        peer = lax.rem(h + e, heads)
        for i, (src, dst, size) in enumerate(
            (
                (q_turn, q_all.at[c, h], q_width),
                (k_turn, k_mine.at[h], width),
                (v_turn, v_mine.at[h], width),
            )
        ):
            swaps.append(
                remote(
                    src.at[:, pl.ds(pl.multiple_of(peer * size, size), size)],
                    dst,
                    swap_send.at[i, e - 1],
                    swap_recv.at[i, e - 1],
                    head=peer,
                )
            )
    for copy in swaps:
        copy.start()
    map_copies = [
        remote(page_map, maps.at[c], map_send.at[e - 1], map_recv.at[e - 1], ctx=lax.rem(c + e, n))
        for e in range(1, n)
    ]
    for copy in map_copies:
        copy.start()
    own_map = pltpu.make_async_copy(page_map, maps.at[c], local_sem.at[5])
    own_map.start()
    for copy in own_turn:
        copy.wait()
    for copy in swaps:
        copy.wait()

    far_q = [
        remote(q_all.at[c], q_all.at[c], far_q_send.at[d - 1], far_q_recv.at[d - 1], ctx=same_core(d))
        for d in range(1, chips)
    ]
    for copy in far_q:
        copy.start()
    near_q = [
        remote(q_all.at[c], q_all.at[c], near_q_send.at[0], near_q_recv.at[0], ctx=sibling)
    ]
    near_q[0].start()

    for copy in pages_in:
        copy.wait()

    def scale_page(j, carry):
        slot = order[j]
        for raw, sent, scale in ((raw_k, sent_k, k_scale), (raw_v, sent_v, v_scale)):
            page = raw[slot]
            for g in range(kv_heads):
                columns = slice(g * head_dim, (g + 1) * head_dim)
                sent[j, :, columns] = (
                    page[:, columns].astype(jnp.float32) * scale[g, slot]
                ).astype(jnp.bfloat16)
        return carry

    lax.fori_loop(0, slots, scale_page, 0)

    page_copies = []
    for e in range(1, n):
        peer = lax.rem(c + e, n)
        for i, (sent, recv) in enumerate(((sent_k, recv_k), (sent_v, recv_v))):
            page_copies.append(
                remote(
                    sent.at[pl.ds(peer * per_peer, per_peer)],
                    recv.at[c],
                    page_send.at[i, e - 1],
                    page_recv.at[i, e - 1],
                    ctx=peer,
                )
            )
    for copy in page_copies:
        copy.start()
    own_pages = [
        pltpu.make_async_copy(
            sent.at[pl.ds(c * per_peer, per_peer)], recv.at[c], local_sem.at[6 + i]
        )
        for i, (sent, recv) in enumerate(((sent_k, recv_k), (sent_v, recv_v)))
    ]
    for copy in own_pages:
        copy.start()

    at_once = max(1, min(per_group, 256 // rows))
    chunks = per_group // at_once
    lanes = lax.broadcasted_iota(jnp.int32, (rows, 128), 1)

    def flat(block):
        if part_rows % 16 == 0:
            return block.reshape(rows, block.shape[2])
        wide = block.astype(jnp.float32)
        return jnp.concatenate([wide[i] for i in range(heads)], axis=0).astype(jnp.bfloat16)

    def attend(block, g, chunk):
        first = g * per_group + chunk * at_once
        start = pl.multiple_of(first * head_dim, head_dim)
        own = pl.ds(pl.multiple_of(g * head_dim, head_dim), head_dim)
        q_block = flat(q_all[block, :, :, pl.ds(start, at_once * head_dim)])
        query = jnp.concatenate(
            [q_block[:, i * head_dim : (i + 1) * head_dim] for i in range(at_once)], axis=0
        )
        keys = sent_k[:, :, own].reshape(slots * page_rows, head_dim)
        values = sent_v[:, :, own].reshape(slots * page_rows, head_dim)
        turn_keys = flat(k_mine[:, :, own])
        turn_values = flat(v_mine[:, :, own])
        cached = lax.dot_general(query, keys, NT, preferred_element_type=jnp.float32)
        recent = lax.dot_general(query, turn_keys, NT, preferred_element_type=jnp.float32)
        line = lax.broadcasted_iota(jnp.int32, (at_once, rows, rows), 1).reshape(
            at_once * rows, rows
        )
        column = lax.broadcasted_iota(jnp.int32, (at_once * rows, rows), 1)
        visible = c * rows + column <= block * rows + line
        recent = jnp.where(visible, recent, -jnp.inf)
        peak = jnp.maximum(
            jnp.max(cached, axis=1, keepdims=True), jnp.max(recent, axis=1, keepdims=True)
        )
        peak = peak * factor
        cached = jnp.exp2(cached * factor - peak).astype(jnp.bfloat16)
        recent = jnp.exp2(recent * factor - peak).astype(jnp.bfloat16)

        def counted(value):
            return jnp.concatenate([value, jnp.ones_like(value)], axis=1)

        both = jnp.dot(cached, counted(values), preferred_element_type=jnp.float32) + jnp.dot(
            recent, counted(turn_values), preferred_element_type=jnp.float32
        )
        mixed, total = both[:, :head_dim], both[:, head_dim : head_dim + 1]
        kept = stats[block]
        for i in range(at_once):
            these = slice(i * rows, (i + 1) * rows)
            acc[block, :, pl.ds(pl.multiple_of(start + i * head_dim, head_dim), head_dim)] = mixed[
                these
            ]
            kept = jnp.where(lanes == first + i, peak[these], kept)
            kept = jnp.where(lanes == q_heads + first + i, total[these], kept)
        stats[block] = kept

    def attend_block(block):
        stats[block] = jnp.zeros((rows, 128), jnp.float32)

        def step(i, carry):
            attend(block, i // chunks, i % chunks)
            return carry

        lax.fori_loop(0, kv_heads * chunks, step, 0)

    near = []

    def give(d):
        block = other_core(d)
        for i, (src, dst) in enumerate(((acc, sib_acc), (stats, sib_stats))):
            copy = remote(
                src.at[block], dst.at[d], near_send.at[i, d], near_recv.at[i, d], ctx=sibling
            )
            copy.start()
            near.append(copy)

    attend_block(c)
    for d in range(1, chips):
        far_q[d - 1].wait()
        source = lax.rem(chip + chips - d, chips) * 2 + core
        near_q.append(
            remote(
                q_all.at[source],
                q_all.at[source],
                near_q_send.at[d],
                near_q_recv.at[d],
                ctx=sibling,
            )
        )
        near_q[d].start()
    near_q[0].wait()
    attend_block(sibling)
    give(0)
    for d in range(1, chips):
        near_q[d].wait()

    def far_other(d, carry):
        attend_block(other_core(d))
        return carry

    def far_same(d, carry):
        attend_block(same_core(d))
        return carry

    lax.fori_loop(1, chips, far_other, 0)
    for d in range(1, chips):
        give(d)
    lax.fori_loop(1, chips, far_same, 0)

    def pick(stat, i):
        return stat[:, i : i + 1], stat[:, q_heads + i : q_heads + i + 1]

    def join(stats_a, read_a, stats_b, read_b, write):
        kept = jnp.zeros((rows, 128), jnp.float32)
        for i in range(q_heads):
            columns = slice(i * head_dim, (i + 1) * head_dim)
            peak_a, total_a = pick(stats_a, i)
            peak_b, total_b = pick(stats_b, i)
            peak = jnp.maximum(peak_a, peak_b)
            weight_a = jnp.exp2(peak_a - peak)
            weight_b = jnp.exp2(peak_b - peak)
            total = total_a * weight_a + total_b * weight_b
            mixed = read_a(columns) * weight_a + read_b(columns).astype(jnp.float32) * weight_b
            write(columns, mixed, total)
            kept = jnp.where(lanes == i, peak, kept)
            kept = jnp.where(lanes == q_heads + i, total, kept)
        return kept

    far = []
    for d in [*range(1, chips), 0]:
        near[2 * d].wait()
        near[2 * d + 1].wait()
        block = same_core(d)

        def write(columns, mixed, total, d=d):
            if d:
                far_out[d - 1, :, columns] = mixed.astype(jnp.bfloat16)
            elif chips == 1:
                out[:, columns] = (mixed / total).astype(jnp.bfloat16)
            else:
                acc[c, :, columns] = mixed

        kept = join(
            stats[block],
            lambda columns, block=block: acc[block, :, columns],
            sib_stats[d],
            lambda columns, d=d: sib_acc[d, :, columns],
            write,
        )
        if d:
            far_out_stats[d - 1] = kept
            for i, (src, dst) in enumerate(((far_out, far_in), (far_out_stats, far_in_stats))):
                copy = remote(
                    src.at[d - 1],
                    dst.at[d - 1],
                    far_send.at[i, d - 1],
                    far_recv.at[i, d - 1],
                    ctx=block,
                )
                copy.start()
                far.append(copy)
        else:
            stats[c] = kept

    for d in range(1, chips):
        far[2 * (d - 1)].wait()
        far[2 * (d - 1) + 1].wait()
        last = d == chips - 1

        def write_far(columns, mixed, total, last=last):
            if last:
                out[:, columns] = (mixed / total).astype(jnp.bfloat16)
            else:
                acc[c, :, columns] = mixed

        kept = join(
            stats[c],
            lambda columns: acc[c, :, columns],
            far_in_stats[d - 1],
            lambda columns, d=d: far_in[d - 1, :, columns],
            write_far,
        )
        if not last:
            stats[c] = kept

    own_map.wait()
    for copy in own_pages + map_copies + page_copies:
        copy.wait()


def place_kernel(n, maps, attn, recv_k, recv_v, out, out_k, out_v, sem):
    c = lax.axis_index("ctx")
    slots = out_k.shape[0]
    half = slots // 2
    passed = pltpu.make_async_copy(attn, out, sem.at[2])
    passed.start()
    for source in range(n):

        def visit(s, count, source=source):
            page = maps[source, 0, s]
            block = page // half
            within = page % half
            first = block == c
            mine = first | (block == 2 * n - 1 - c)

            @pl.when(mine)
            def _():
                place = jnp.where(first, within, half + within)
                for recv, to, i in ((recv_k, out_k, 0), (recv_v, out_v, 1)):
                    pltpu.make_async_copy(recv.at[source, count], to.at[place], sem.at[i]).start()

            return count + mine.astype(jnp.int32)

        lax.fori_loop(0, slots, visit, jnp.int32(0))
    passed.wait()
    for to, i in ((out_k, 0), (out_v, 1)):
        pltpu.make_async_copy(to, to, sem.at[i]).wait()


def local(q_turn, k_turn, v_turn, cache_k, cache_v, k_scale, v_scale, page_map):
    n = lax.axis_size("ctx")
    heads = lax.axis_size("head")
    slots, page_rows, width = cache_k.shape
    kv_heads = k_scale.shape[1]
    head_dim = width // kv_heads
    part_rows = q_turn.shape[0]
    rows = part_rows * heads
    q_width = q_turn.shape[1] // heads
    half = slots // 2
    per_peer = slots // n
    chips = n // 2
    bf16, f32 = jnp.bfloat16, jnp.float32

    block = page_map // half
    owner = jnp.where(block < n, block, 2 * n - 1 - block)
    slot = jnp.arange(slots, dtype=jnp.int32)
    before = (owner[None, :] == owner[:, None]) & (slot[None, :] < slot[:, None])
    rank = owner * per_peer + jnp.sum(before, axis=1, dtype=jnp.int32)
    order = jnp.sum(
        jnp.where(rank[None, :] == slot[:, None], slot[None, :], 0), axis=1, dtype=jnp.int32
    )
    map_row = jnp.pad(page_map, (0, -slots % 128))[None, :]

    smem = pl.BlockSpec(memory_space=pltpu.SMEM)
    vmem = pl.BlockSpec(memory_space=pltpu.VMEM)
    anywhere = pl.BlockSpec(memory_space=pl.ANY)
    hbm = pl.BlockSpec(memory_space=pltpu.HBM)
    dma = pltpu.SemaphoreType.DMA
    received = jax.ShapeDtypeStruct((n, per_peer, page_rows, width), bf16)
    some = max(1, chips - 1)
    keys = slots * page_rows + rows
    attn, recv_k, recv_v, maps = pl.pallas_call(
        functools.partial(main_kernel, n, heads, head_dim),
        out_shape=(
            jax.ShapeDtypeStruct((rows, q_width), bf16),
            received,
            received,
            jax.ShapeDtypeStruct((n, *map_row.shape), jnp.int32),
        ),
        in_specs=[smem] * 3 + [vmem] + [hbm] * 5,
        out_specs=(vmem, vmem, vmem, vmem),
        scratch_shapes=[
            pltpu.VMEM((slots, page_rows, width), bf16),
            pltpu.VMEM((slots, page_rows, width), bf16),
            pltpu.VMEM((slots, page_rows, width), bf16),
            pltpu.VMEM((slots, page_rows, width), bf16),
            pltpu.VMEM((n, heads, part_rows, q_width), bf16),
            pltpu.VMEM((heads, part_rows, width), bf16),
            pltpu.VMEM((heads, part_rows, width), bf16),
            pltpu.VMEM((n, rows, q_width), f32),
            pltpu.VMEM((n, rows, 128), f32),
            pltpu.VMEM((chips, rows, q_width), f32),
            pltpu.VMEM((chips, rows, 128), f32),
            pltpu.VMEM((some, rows, q_width), bf16),
            pltpu.VMEM((some, rows, 128), f32),
            pltpu.VMEM((some, rows, q_width), bf16),
            pltpu.VMEM((some, rows, 128), f32),
            dma((8,)),
            dma((3, max(1, heads - 1))),
            dma((3, max(1, heads - 1))),
            dma((some,)),
            dma((some,)),
            dma((chips,)),
            dma((chips,)),
            dma((2, n - 1)),
            dma((2, n - 1)),
            dma((n - 1,)),
            dma((n - 1,)),
            dma((2, chips)),
            dma((2, chips)),
            dma((2, some)),
            dma((2, some)),
        ],
        compiler_params=pltpu.CompilerParams(
            collective_id=0, has_side_effects=True, vmem_limit_bytes=48 * 2**20
        ),
        cost_estimate=pl.CostEstimate(
            flops=4 * n * rows * q_width * keys,
            bytes_accessed=8 * slots * page_rows * width * 2,
            transcendentals=n * rows * (q_width // head_dim) * keys,
        ),
        name="exchange_and_attend",
    )(order, k_scale.T, v_scale.T, map_row, q_turn, k_turn, v_turn, cache_k, cache_v)

    paged = jax.ShapeDtypeStruct((slots, page_rows, width), bf16)
    attn_out, paired_k, paired_v = pl.pallas_call(
        functools.partial(place_kernel, n),
        out_shape=(jax.ShapeDtypeStruct((rows, q_width), bf16), paged, paged),
        in_specs=[smem, anywhere, anywhere, anywhere],
        out_specs=(hbm, hbm, hbm),
        scratch_shapes=[dma((3,))],
        compiler_params=pltpu.CompilerParams(vmem_limit_bytes=2 * 2**20),
        cost_estimate=pl.CostEstimate(
            flops=0, bytes_accessed=4 * slots * page_rows * width * 2, transcendentals=0
        ),
        name="place_pages",
    )(maps, attn, recv_k, recv_v)
    flat = (slots * page_rows, width)
    return (attn_out, paired_k.reshape(flat), paired_v.reshape(flat))


def solution(mesh):
    return jax.shard_map(
        local,
        mesh=mesh,
        in_specs=(
            P(("rep", "ctx", "head"), None),
            P(("rep", "ctx", "head"), None),
            P(("rep", "ctx", "head"), None),
            P(("rep", "ctx"), None, "head"),
            P(("rep", "ctx"), None, "head"),
            P(("rep", "ctx"), "head"),
            P(("rep", "ctx"), "head"),
            P(("rep", "ctx")),
        ),
        out_specs=(P(("rep", "ctx"), "head"), P(("rep", "ctx"), "head"), P(("rep", "ctx"), "head")),
        check_vma=False,
    )
```

```python
import functools
import math

import jax
import jax.numpy as jnp
from jax import lax
from jax.experimental import pallas as pl
from jax.experimental.pallas import tpu as pltpu
from jax.sharding import PartitionSpec as P

MESH = pl.DeviceIdType.MESH
NT = (((1,), (1,)), ((), ()))


def main_kernel(
    n,
    heads,
    head_dim,
    order,
    k_scale,
    v_scale,
    page_map,
    q_turn,
    k_turn,
    v_turn,
    cache_k,
    cache_v,
    out,
    recv_k,
    recv_v,
    maps,
    raw_k,
    raw_v,
    sent_k,
    sent_v,
    q_all,
    k_mine,
    v_mine,
    acc,
    stats,
    sib_acc,
    sib_stats,
    far_out,
    far_out_stats,
    far_in,
    far_in_stats,
    local_sem,
    swap_send,
    swap_recv,
    far_q_send,
    far_q_recv,
    near_q_send,
    near_q_recv,
    page_send,
    page_recv,
    map_send,
    map_recv,
    near_send,
    near_recv,
    far_send,
    far_recv,
):
    c = lax.axis_index("ctx")
    h = lax.axis_index("head")
    chips = n // 2
    chip, core = c // 2, c % 2
    sibling = chip * 2 + (1 - core)
    slots, page_rows, width = raw_k.shape
    per_peer = slots // n
    part_rows, q_width = q_all.shape[2], q_all.shape[3]
    rows = heads * part_rows
    kv_heads = width // head_dim
    q_heads = q_width // head_dim
    per_group = q_heads // kv_heads
    factor = math.log2(math.e) / math.sqrt(head_dim)

    def remote(src, dst, send, recv, **where):
        return pltpu.make_async_remote_copy(
            src_ref=src,
            dst_ref=dst,
            send_sem=send,
            recv_sem=recv,
            device_id=where,
            device_id_type=MESH,
        )

    def same_core(d):
        return lax.rem(chip + d, chips) * 2 + core

    def other_core(d):
        return lax.rem(chip + d, chips) * 2 + (1 - core)

    pages_in = [
        pltpu.make_async_copy(cache_k, raw_k, local_sem.at[0]),
        pltpu.make_async_copy(cache_v, raw_v, local_sem.at[1]),
    ]
    for copy in pages_in:
        copy.start()
    own_turn = [
        pltpu.make_async_copy(
            src.at[:, pl.ds(pl.multiple_of(h * size, size), size)], dst, local_sem.at[2 + i]
        )
        for i, (src, dst, size) in enumerate(
            (
                (q_turn, q_all.at[c, h], q_width),
                (k_turn, k_mine.at[h], width),
                (v_turn, v_mine.at[h], width),
            )
        )
    ]
    for copy in own_turn:
        copy.start()

    barrier = pltpu.get_barrier_semaphore()
    for e in range(1, n):
        pl.semaphore_signal(
            barrier, inc=1, device_id={"ctx": lax.rem(c + e, n)}, device_id_type=MESH
        )
    for e in range(1, heads):
        pl.semaphore_signal(
            barrier, inc=1, device_id={"head": lax.rem(h + e, heads)}, device_id_type=MESH
        )
    pl.semaphore_wait(barrier, n - 1 + heads - 1)

    swaps = []
    for e in range(1, heads):
        peer = lax.rem(h + e, heads)
        for i, (src, dst, size) in enumerate(
            (
                (q_turn, q_all.at[c, h], q_width),
                (k_turn, k_mine.at[h], width),
                (v_turn, v_mine.at[h], width),
            )
        ):
            swaps.append(
                remote(
                    src.at[:, pl.ds(pl.multiple_of(peer * size, size), size)],
                    dst,
                    swap_send.at[i, e - 1],
                    swap_recv.at[i, e - 1],
                    head=peer,
                )
            )
    for copy in swaps:
        copy.start()
    map_copies = [
        remote(page_map, maps.at[c], map_send.at[e - 1], map_recv.at[e - 1], ctx=lax.rem(c + e, n))
        for e in range(1, n)
    ]
    for copy in map_copies:
        copy.start()
    own_map = pltpu.make_async_copy(page_map, maps.at[c], local_sem.at[5])
    own_map.start()
    for copy in own_turn:
        copy.wait()
    for copy in swaps:
        copy.wait()

    far_q = [
        remote(q_all.at[c], q_all.at[c], far_q_send.at[d - 1], far_q_recv.at[d - 1], ctx=same_core(d))
        for d in range(1, chips)
    ]
    for copy in far_q:
        copy.start()
    near_q = [
        remote(q_all.at[c], q_all.at[c], near_q_send.at[0], near_q_recv.at[0], ctx=sibling)
    ]
    near_q[0].start()

    for copy in pages_in:
        copy.wait()

    def scale_page(j, carry):
        slot = order[j]
        for raw, sent, scale in ((raw_k, sent_k, k_scale), (raw_v, sent_v, v_scale)):
            page = raw[slot]
            for g in range(kv_heads):
                columns = slice(g * head_dim, (g + 1) * head_dim)
                sent[j, :, columns] = (
                    page[:, columns].astype(jnp.float32) * scale[g, slot]
                ).astype(jnp.bfloat16)
        return carry

    lax.fori_loop(0, slots, scale_page, 0)

    page_copies = []
    for e in range(1, n):
        peer = lax.rem(c + e, n)
        for i, (sent, recv) in enumerate(((sent_k, recv_k), (sent_v, recv_v))):
            page_copies.append(
                remote(
                    sent.at[pl.ds(peer * per_peer, per_peer)],
                    recv.at[c],
                    page_send.at[i, e - 1],
                    page_recv.at[i, e - 1],
                    ctx=peer,
                )
            )
    for copy in page_copies:
        copy.start()
    own_pages = [
        pltpu.make_async_copy(
            sent.at[pl.ds(c * per_peer, per_peer)], recv.at[c], local_sem.at[6 + i]
        )
        for i, (sent, recv) in enumerate(((sent_k, recv_k), (sent_v, recv_v)))
    ]
    for copy in own_pages:
        copy.start()

    at_once = max(1, min(per_group, 256 // rows))
    chunks = per_group // at_once
    paired = 2 if kv_heads * chunks % 2 == 0 else 1
    lanes = lax.broadcasted_iota(jnp.int32, (rows, 128), 1)

    def flat(block):
        if part_rows % 16 == 0:
            return block.reshape(rows, block.shape[2])
        wide = block.astype(jnp.float32)
        return jnp.concatenate([wide[i] for i in range(heads)], axis=0).astype(jnp.bfloat16)

    def scores(block, i):
        g, chunk = i // chunks, i % chunks
        first = g * per_group + chunk * at_once
        start = pl.multiple_of(first * head_dim, head_dim)
        own = pl.ds(pl.multiple_of(g * head_dim, head_dim), head_dim)
        q_block = flat(q_all[block, :, :, pl.ds(start, at_once * head_dim)])
        query = jnp.concatenate(
            [q_block[:, i * head_dim : (i + 1) * head_dim] for i in range(at_once)], axis=0
        )
        keys = sent_k[:, :, own].reshape(slots * page_rows, head_dim)
        turn_keys = flat(k_mine[:, :, own])
        cached = lax.dot_general(query, keys, NT, preferred_element_type=jnp.float32)
        recent = lax.dot_general(query, turn_keys, NT, preferred_element_type=jnp.float32)
        return first, start, own, cached, recent

    def finish(block, first, start, own, cached, recent):
        values = sent_v[:, :, own].reshape(slots * page_rows, head_dim)
        turn_values = flat(v_mine[:, :, own])
        line = lax.broadcasted_iota(jnp.int32, (at_once, rows, rows), 1).reshape(
            at_once * rows, rows
        )
        column = lax.broadcasted_iota(jnp.int32, (at_once * rows, rows), 1)
        visible = c * rows + column <= block * rows + line
        recent = jnp.where(visible, recent, -jnp.inf)
        peak = jnp.maximum(
            jnp.max(cached, axis=1, keepdims=True), jnp.max(recent, axis=1, keepdims=True)
        )
        peak = peak * factor
        cached = jnp.exp2(cached * factor - peak).astype(jnp.bfloat16)
        recent = jnp.exp2(recent * factor - peak).astype(jnp.bfloat16)

        def counted(value):
            return jnp.concatenate([value, jnp.ones_like(value)], axis=1)

        both = jnp.dot(cached, counted(values), preferred_element_type=jnp.float32) + jnp.dot(
            recent, counted(turn_values), preferred_element_type=jnp.float32
        )
        mixed, total = both[:, :head_dim], both[:, head_dim : head_dim + 1]
        kept = stats[block]
        for i in range(at_once):
            these = slice(i * rows, (i + 1) * rows)
            acc[block, :, pl.ds(pl.multiple_of(start + i * head_dim, head_dim), head_dim)] = mixed[
                these
            ]
            kept = jnp.where(lanes == first + i, peak[these], kept)
            kept = jnp.where(lanes == q_heads + first + i, total[these], kept)
        stats[block] = kept

    def attend_block(block):
        stats[block] = jnp.zeros((rows, 128), jnp.float32)

        def step(i, carry):
            ready = [scores(block, i * paired + k) for k in range(paired)]
            for one in ready:
                finish(block, *one)
            return carry

        lax.fori_loop(0, kv_heads * chunks // paired, step, 0)

    near = {}

    def give(d):
        block = other_core(d)
        near[d] = []
        for i, (src, dst) in enumerate(((acc, sib_acc), (stats, sib_stats))):
            copy = remote(
                src.at[block], dst.at[d], near_send.at[i, d], near_recv.at[i, d], ctx=sibling
            )
            copy.start()
            near[d].append(copy)

    attend_block(c)
    for d in range(1, chips):
        far_q[d - 1].wait()
        source = lax.rem(chip + chips - d, chips) * 2 + core
        near_q.append(
            remote(
                q_all.at[source],
                q_all.at[source],
                near_q_send.at[d],
                near_q_recv.at[d],
                ctx=sibling,
            )
        )
        near_q[d].start()
    for d in range(1, chips):
        near_q[d].wait()

    def far_other(d, carry):
        attend_block(other_core(d))
        return carry

    def far_same(d, carry):
        attend_block(same_core(d))
        return carry

    lax.fori_loop(1, chips, far_other, 0)
    for d in range(1, chips):
        give(d)
    lax.fori_loop(1, chips, far_same, 0)

    def pick(stat, i):
        return stat[:, i : i + 1], stat[:, q_heads + i : q_heads + i + 1]

    def join(stats_a, read_a, stats_b, read_b, write):
        kept = jnp.zeros((rows, 128), jnp.float32)
        for i in range(q_heads):
            columns = slice(i * head_dim, (i + 1) * head_dim)
            peak_a, total_a = pick(stats_a, i)
            peak_b, total_b = pick(stats_b, i)
            peak = jnp.maximum(peak_a, peak_b)
            weight_a = jnp.exp2(peak_a - peak)
            weight_b = jnp.exp2(peak_b - peak)
            total = total_a * weight_a + total_b * weight_b
            mixed = read_a(columns) * weight_a + read_b(columns).astype(jnp.float32) * weight_b
            write(columns, mixed, total)
            kept = jnp.where(lanes == i, peak, kept)
            kept = jnp.where(lanes == q_heads + i, total, kept)
        return kept

    far = []
    for d in [*range(1, chips), 0]:
        if d == 0:
            near_q[0].wait()
            attend_block(sibling)
            give(0)
        for copy in near[d]:
            copy.wait()
        block = same_core(d)

        def write(columns, mixed, total, d=d):
            if d:
                far_out[d - 1, :, columns] = mixed.astype(jnp.bfloat16)
            elif chips == 1:
                out[:, columns] = (mixed / total).astype(jnp.bfloat16)
            else:
                acc[c, :, columns] = mixed

        kept = join(
            stats[block],
            lambda columns, block=block: acc[block, :, columns],
            sib_stats[d],
            lambda columns, d=d: sib_acc[d, :, columns],
            write,
        )
        if d:
            far_out_stats[d - 1] = kept
            for i, (src, dst) in enumerate(((far_out, far_in), (far_out_stats, far_in_stats))):
                copy = remote(
                    src.at[d - 1],
                    dst.at[d - 1],
                    far_send.at[i, d - 1],
                    far_recv.at[i, d - 1],
                    ctx=block,
                )
                copy.start()
                far.append(copy)
        else:
            stats[c] = kept

    for d in range(1, chips):
        far[2 * (d - 1)].wait()
        far[2 * (d - 1) + 1].wait()
        last = d == chips - 1

        def write_far(columns, mixed, total, last=last):
            if last:
                out[:, columns] = (mixed / total).astype(jnp.bfloat16)
            else:
                acc[c, :, columns] = mixed

        kept = join(
            stats[c],
            lambda columns: acc[c, :, columns],
            far_in_stats[d - 1],
            lambda columns, d=d: far_in[d - 1, :, columns],
            write_far,
        )
        if not last:
            stats[c] = kept

    own_map.wait()
    for copy in own_pages + map_copies + page_copies:
        copy.wait()


def place_kernel(n, maps, attn, recv_k, recv_v, out, out_k, out_v, sem):
    c = lax.axis_index("ctx")
    slots = out_k.shape[0]
    half = slots // 2
    passed = pltpu.make_async_copy(attn, out, sem.at[2])
    passed.start()
    for source in range(n):

        def visit(s, count, source=source):
            page = maps[source, 0, s]
            block = page // half
            within = page % half
            first = block == c
            mine = first | (block == 2 * n - 1 - c)

            @pl.when(mine)
            def _():
                place = jnp.where(first, within, half + within)
                for recv, to, i in ((recv_k, out_k, 0), (recv_v, out_v, 1)):
                    pltpu.make_async_copy(recv.at[source, count], to.at[place], sem.at[i]).start()

            return count + mine.astype(jnp.int32)

        lax.fori_loop(0, slots, visit, jnp.int32(0))
    passed.wait()
    for to, i in ((out_k, 0), (out_v, 1)):
        pltpu.make_async_copy(to, to, sem.at[i]).wait()


def local(q_turn, k_turn, v_turn, cache_k, cache_v, k_scale, v_scale, page_map):
    n = lax.axis_size("ctx")
    heads = lax.axis_size("head")
    slots, page_rows, width = cache_k.shape
    kv_heads = k_scale.shape[1]
    head_dim = width // kv_heads
    part_rows = q_turn.shape[0]
    rows = part_rows * heads
    q_width = q_turn.shape[1] // heads
    half = slots // 2
    per_peer = slots // n
    chips = n // 2
    bf16, f32 = jnp.bfloat16, jnp.float32

    block = page_map // half
    owner = jnp.where(block < n, block, 2 * n - 1 - block)
    slot = jnp.arange(slots, dtype=jnp.int32)
    before = (owner[None, :] == owner[:, None]) & (slot[None, :] < slot[:, None])
    rank = owner * per_peer + jnp.sum(before, axis=1, dtype=jnp.int32)
    order = jnp.sum(
        jnp.where(rank[None, :] == slot[:, None], slot[None, :], 0), axis=1, dtype=jnp.int32
    )
    map_row = jnp.pad(page_map, (0, -slots % 128))[None, :]

    smem = pl.BlockSpec(memory_space=pltpu.SMEM)
    vmem = pl.BlockSpec(memory_space=pltpu.VMEM)
    anywhere = pl.BlockSpec(memory_space=pl.ANY)
    hbm = pl.BlockSpec(memory_space=pltpu.HBM)
    dma = pltpu.SemaphoreType.DMA
    received = jax.ShapeDtypeStruct((n, per_peer, page_rows, width), bf16)
    some = max(1, chips - 1)
    keys = slots * page_rows + rows
    attn, recv_k, recv_v, maps = pl.pallas_call(
        functools.partial(main_kernel, n, heads, head_dim),
        out_shape=(
            jax.ShapeDtypeStruct((rows, q_width), bf16),
            received,
            received,
            jax.ShapeDtypeStruct((n, *map_row.shape), jnp.int32),
        ),
        in_specs=[smem] * 3 + [vmem] + [hbm] * 5,
        out_specs=(vmem, vmem, vmem, vmem),
        scratch_shapes=[
            pltpu.VMEM((slots, page_rows, width), bf16),
            pltpu.VMEM((slots, page_rows, width), bf16),
            pltpu.VMEM((slots, page_rows, width), bf16),
            pltpu.VMEM((slots, page_rows, width), bf16),
            pltpu.VMEM((n, heads, part_rows, q_width), bf16),
            pltpu.VMEM((heads, part_rows, width), bf16),
            pltpu.VMEM((heads, part_rows, width), bf16),
            pltpu.VMEM((n, rows, q_width), f32),
            pltpu.VMEM((n, rows, 128), f32),
            pltpu.VMEM((chips, rows, q_width), f32),
            pltpu.VMEM((chips, rows, 128), f32),
            pltpu.VMEM((some, rows, q_width), bf16),
            pltpu.VMEM((some, rows, 128), f32),
            pltpu.VMEM((some, rows, q_width), bf16),
            pltpu.VMEM((some, rows, 128), f32),
            dma((8,)),
            dma((3, max(1, heads - 1))),
            dma((3, max(1, heads - 1))),
            dma((some,)),
            dma((some,)),
            dma((chips,)),
            dma((chips,)),
            dma((2, n - 1)),
            dma((2, n - 1)),
            dma((n - 1,)),
            dma((n - 1,)),
            dma((2, chips)),
            dma((2, chips)),
            dma((2, some)),
            dma((2, some)),
        ],
        compiler_params=pltpu.CompilerParams(
            collective_id=0, has_side_effects=True, vmem_limit_bytes=48 * 2**20
        ),
        cost_estimate=pl.CostEstimate(
            flops=4 * n * rows * q_width * keys,
            bytes_accessed=8 * slots * page_rows * width * 2,
            transcendentals=n * rows * (q_width // head_dim) * keys,
        ),
        name="exchange_and_attend",
    )(order, k_scale.T, v_scale.T, map_row, q_turn, k_turn, v_turn, cache_k, cache_v)

    paged = jax.ShapeDtypeStruct((slots, page_rows, width), bf16)
    attn_out, paired_k, paired_v = pl.pallas_call(
        functools.partial(place_kernel, n),
        out_shape=(jax.ShapeDtypeStruct((rows, q_width), bf16), paged, paged),
        in_specs=[smem, anywhere, anywhere, anywhere],
        out_specs=(hbm, hbm, hbm),
        scratch_shapes=[dma((3,))],
        compiler_params=pltpu.CompilerParams(vmem_limit_bytes=2 * 2**20),
        cost_estimate=pl.CostEstimate(
            flops=0, bytes_accessed=4 * slots * page_rows * width * 2, transcendentals=0
        ),
        name="place_pages",
    )(maps, attn, recv_k, recv_v)
    flat = (slots * page_rows, width)
    return (attn_out, paired_k.reshape(flat), paired_v.reshape(flat))


def solution(mesh):
    return jax.shard_map(
        local,
        mesh=mesh,
        in_specs=(
            P(("rep", "ctx", "head"), None),
            P(("rep", "ctx", "head"), None),
            P(("rep", "ctx", "head"), None),
            P(("rep", "ctx"), None, "head"),
            P(("rep", "ctx"), None, "head"),
            P(("rep", "ctx"), "head"),
            P(("rep", "ctx"), "head"),
            P(("rep", "ctx")),
        ),
        out_specs=(P(("rep", "ctx"), "head"), P(("rep", "ctx"), "head"), P(("rep", "ctx"), "head")),
        check_vma=False,
    )
```
